32 devices in a mesh: dp: 32 (over z, y, x, core).
Axes of the slice: x: 2, y: 2, z: 4, core: 2. Of those that a mesh axis runs over, the one named last changes fastest.
Arguments:
- grads: bfloat16 [32, 512, 128], P('dp'), may hold values from -3200 to 3200
- master: float32 [512, 128], P('dp'), may hold values from -6 to 6
- first_q: bfloat16 [512, 128], P('dp'), may hold values from -1 to 1
- first_scale: float32 [512], P('dp'), may hold values from 0.005 to 0.05
- second_q: bfloat16 [512, 128], P('dp'), may hold values from 0.099609375 to 1
- second_scale: float32 [512], P('dp'), may hold values from 2e-05 to 0.0002
Outputs:
- weights: bfloat16 [512, 128], replicated
- master_new: float32 [512, 128], P('dp')
- first_q_new: bfloat16 [512, 128], P('dp')
- first_scale_new: float32 [512], P('dp')
- second_q_new: bfloat16 [512, 128], P('dp')
- second_scale_new: float32 [512], P('dp')
The draws below stay inside these ranges and needn't reach their ends.
All inputs are finite; a program needn't handle non-finite values. Where the reference program divides by a largest or mean magnitude, that divisor is 1e-20 or more.
Results may differ from the reference program's by a relative error of at most 0.001.
Values may be sent and summed in bfloat16 or wider, within the bound.
A program may use at most 64 MiB of HBM per device.

```python
import math
import jax
import jax.numpy as jnp
from jax import lax

D = 6144
BLK_DEV = 16
BLOCKS = 512
N_DP = 32


def draw_grads(key, part):
    keys = jax.random.split(jax.random.fold_in(key, 17), 4)
    lane_groups = D // 128
    block_ids = jnp.arange(BLOCKS)
    row_ids = block_ids // lane_groups
    row_count = (BLOCKS + lane_groups - 1) // lane_groups
    row_scale = 10.0 ** (row_ids.astype(jnp.float32) / max(row_count - 1, 1))
    column_scale = 10.0 ** jax.random.uniform(keys[0], (lane_groups, 128), jnp.float32)
    block_cols = column_scale[block_ids % lane_groups]
    replica_scale = 2.0 ** jax.random.uniform(keys[1], (N_DP,), jnp.float32, -1.0, 1.0)
    owners = jax.random.permutation(keys[2], N_DP)
    spike = jnp.where((block_ids // BLK_DEV)[None, :] == owners[:, None], 4.0, 1.0)
    noise = jnp.clip(jax.random.normal(keys[3], (N_DP, BLOCKS, 128), jnp.float32), -4.0, 4.0)
    values = noise * row_scale[None, :, None] * block_cols[None] * replica_scale[:, None, None] * spike[:, :, None]
    return values.astype(jnp.bfloat16)


def block_scale(stream_key, shape, pieces, least, largest):
    loudness = 1.0
    for dim, parts in pieces:
        heights = jax.random.uniform(jax.random.fold_in(jax.random.fold_in(stream_key, 6), dim), (parts,), jnp.float32, least / len(pieces), largest / len(pieces))
        loudness = loudness * jnp.repeat(jnp.exp(heights), shape[dim] // parts).reshape((-1,) + (1,) * (len(shape) - 1 - dim))
    return loudness


def gaussian(rng, dims, deviation, reach, pieces=(), dtype=jnp.bfloat16):
    array = jax.random.normal(rng, dims, jnp.float32) * deviation
    if len(pieces) > 0:
        array = block_scale(rng, dims, pieces, -0.22, 0.18) * array
    return jnp.clip(array, min=-reach, max=reach).astype(dtype)


def setup_inputs(seed: int = 0) -> dict:
    key_list = jax.random.split(jax.random.key(seed), 7)
    return {
        "grads": draw_grads(jax.random.fold_in(key_list[6], 71), 0),
        "master": gaussian(key_list[1], (BLOCKS, 128), 1.0, 6.0, ((0, 32),), jnp.float32),
        "first_q": jnp.clip(jax.random.uniform(key_list[2], (BLOCKS, 128), jnp.float32, -1.0, 1.0) * block_scale(key_list[2], (BLOCKS, 128), ((0, 32),), -0.4, 0.0), -1.0, 1.0).astype(jnp.bfloat16),
        "first_scale": jnp.clip(jnp.exp(math.log(0.05) - 2.3025851 * jax.random.uniform(key_list[3], (BLOCKS,), jnp.float32) ** block_scale(key_list[3], (BLOCKS,), ((0, 32),), -0.2, 0.2)), 0.005, 0.05),
        "second_q": jnp.clip(0.099609375 + 0.9003906 * jax.random.uniform(key_list[4], (BLOCKS, 128), jnp.float32) ** block_scale(key_list[4], (BLOCKS, 128), ((0, 32),), -0.2, 0.2), 0.099609375, 1.0).astype(jnp.bfloat16),
        "second_scale": jnp.clip(jnp.exp(math.log(0.0002) - 2.3025851 * jax.random.uniform(key_list[5], (BLOCKS,), jnp.float32) ** block_scale(key_list[5], (BLOCKS,), ((0, 32),), -0.2, 0.2)), 1.9999999494757503e-05, 0.0002),
    }


beta_one = 0.9
beta_two = 0.95
learn_rate = 0.05
decay_rate = 0.1
adam_epsilon = 1e-08
clip_rms = 0.01
first_fix = 1.0 - 0.9 ** 10
second_fix = 1.0 - 0.95 ** 10

def reference(grads, master, first_q, first_scale, second_q, second_scale):

    def accumulate(carry, piece):
        return (carry + piece.astype(jnp.float32), None)
    start = jnp.zeros(grads.shape[1:], jnp.float32)
    total, _ = lax.scan(accumulate, start, grads)
    norm = jnp.sqrt(jnp.sum(total * total))
    limit = clip_rms * jnp.sqrt(jnp.float32(total.shape[0] * total.shape[1]))
    factor = jnp.minimum(1.0, limit / (norm + 1e-06))
    clipped = factor * total
    first = first_q.astype(jnp.float32) * first_scale[:, None]
    second = second_q.astype(jnp.float32) * second_scale[:, None]
    first_new = beta_one * first + (1.0 - beta_one) * clipped
    second_new = beta_two * second + (1.0 - beta_two) * clipped * clipped
    change = first_new / first_fix / (jnp.sqrt(second_new / second_fix) + adam_epsilon)
    master_new = master * (1.0 - learn_rate * decay_rate) - learn_rate * change
    first_scale_new = lax.optimization_barrier(jnp.max(jnp.abs(first_new), axis=1)) + 1e-08
    second_scale_new = lax.optimization_barrier(jnp.max(jnp.abs(second_new), axis=1)) + 1e-08
    first_q_new = (first_new / first_scale_new[:, None]).astype(jnp.bfloat16)
    second_q_new = (second_new / second_scale_new[:, None]).astype(jnp.bfloat16)
    weights = master_new.astype(jnp.bfloat16)
    return (weights, master_new, first_q_new, first_scale_new, second_q_new, second_scale_new)
```

```python
import functools

import jax
import jax.numpy as jnp
from jax import lax
from jax.experimental import pallas as pl
from jax.experimental.pallas import tpu as pltpu
from jax.sharding import PartitionSpec as P

MESH = pl.DeviceIdType.MESH

beta_one = 0.9
beta_two = 0.95
learn_rate = 0.05
decay_rate = 0.1
adam_epsilon = 1e-08
clip_rms = 0.01
first_fix = 1.0 - 0.9**10
second_fix = 1.0 - 0.95**10


def column_of(row, count):
    down = lax.broadcasted_iota(jnp.int32, (count, count), 0)
    along = lax.broadcasted_iota(jnp.int32, (count, count), 1)
    spread = jnp.broadcast_to(row, (count, count))
    return jnp.sum(jnp.where(down == along, spread, 0.0), axis=1, keepdims=True)


def row_of(column, count):
    down = lax.broadcasted_iota(jnp.int32, (count, count), 0)
    along = lax.broadcasted_iota(jnp.int32, (count, count), 1)
    spread = jnp.broadcast_to(column, (count, count))
    return jnp.sum(jnp.where(down == along, spread, 0.0), axis=0, keepdims=True)


def step_kernel(
    n,
    entries,
    grads_ref,
    master_ref,
    first_q_ref,
    first_scale_ref,
    second_q_ref,
    second_scale_ref,
    weights_ref,
    master_new_ref,
    first_q_new_ref,
    first_scale_new_ref,
    second_q_new_ref,
    second_scale_new_ref,
    local,
    arrived,
    squares,
    mine,
    stage_sem,
    keep_sem,
    grad_send,
    grad_recv,
    norm_send,
    norm_recv,
    gather_send,
    gather_recv,
):
    me = lax.axis_index("dp")
    own = master_ref.shape[0]
    width = master_ref.shape[1]

    stage = pltpu.make_async_copy(grads_ref.at[0], local, stage_sem)
    stage.start()

    barrier = pltpu.get_barrier_semaphore()

    def greet(k, carry):
        pl.semaphore_signal(barrier, inc=1, device_id=(lax.rem(me + k, n),), device_id_type=MESH)
        return carry

    lax.fori_loop(1, n, greet, 0)
    stage.wait()
    pl.semaphore_wait(barrier, n - 1)

    def send_grad(k, carry):
        to = lax.rem(me + k, n)
        pltpu.make_async_remote_copy(
            src_ref=local.at[pl.ds(pl.multiple_of(to * own, own), own)],
            dst_ref=arrived.at[k - 1],
            send_sem=grad_send,
            recv_sem=grad_recv,
            device_id=(to,),
            device_id_type=MESH,
        ).start()
        return carry

    lax.fori_loop(1, n, send_grad, 0)

    total = local[pl.ds(pl.multiple_of(me * own, own), own), :].astype(jnp.float32)
    pltpu.make_async_copy(arrived, arrived, grad_recv).wait()
    total = total + jnp.sum(arrived[...].astype(jnp.float32), axis=0)

    squares[pl.ds(n - 1, 1), :] = jnp.sum(total * total, axis=0, keepdims=True)

    def send_norm(k, carry):
        pltpu.make_async_remote_copy(
            src_ref=squares.at[pl.ds(n - 1, 1)],
            dst_ref=squares.at[pl.ds(k - 1, 1)],
            send_sem=norm_send,
            recv_sem=norm_recv,
            device_id=(lax.rem(me + k, n),),
            device_id_type=MESH,
        ).start()
        return carry

    lax.fori_loop(1, n, send_norm, 0)

    first = first_q_ref[...].astype(jnp.float32) * column_of(first_scale_ref[...], own)
    second = second_q_ref[...].astype(jnp.float32) * column_of(second_scale_ref[...], own)
    kept = master_ref[...] * (1.0 - learn_rate * decay_rate)
    others = squares.at[pl.ds(0, n - 1)]
    pltpu.make_async_copy(others, others, norm_recv).wait()
    norm = jnp.sqrt(jnp.sum(squares[...], keepdims=True))
    limit = clip_rms * jnp.sqrt(jnp.float32(entries))
    factor = jnp.minimum(1.0, limit / (norm + 1e-06))
    clipped = factor * total
    first_new = beta_one * first + (1.0 - beta_one) * clipped
    second_new = beta_two * second + (1.0 - beta_two) * clipped * clipped
    change = first_new / first_fix / (jnp.sqrt(second_new / second_fix) + adam_epsilon)
    master_new = kept - learn_rate * change
    mine[...] = master_new.astype(jnp.bfloat16)

    slot = weights_ref.at[pl.ds(pl.multiple_of(me * own, own), own)]

    def send_weights(k, carry):
        pltpu.make_async_remote_copy(
            src_ref=mine,
            dst_ref=slot,
            send_sem=gather_send,
            recv_sem=gather_recv,
            device_id=(lax.rem(me + k, n),),
            device_id_type=MESH,
        ).start()
        return carry

    lax.fori_loop(1, n, send_weights, 0)
    keep = pltpu.make_async_copy(mine, slot, keep_sem)
    keep.start()

    master_new_ref[...] = master_new
    first_top = jnp.max(jnp.abs(first_new), axis=1, keepdims=True) + 1e-08
    second_top = jnp.max(jnp.abs(second_new), axis=1, keepdims=True) + 1e-08
    first_q_new_ref[...] = (first_new / first_top).astype(jnp.bfloat16)
    second_q_new_ref[...] = (second_new / second_top).astype(jnp.bfloat16)
    first_scale_new_ref[...] = row_of(first_top, own)
    second_scale_new_ref[...] = row_of(second_top, own)

    keep.wait()
    sent = local.at[pl.ds(0, (n - 1) * own)]
    gathered = weights_ref.at[pl.ds(0, (n - 1) * own)]
    pltpu.make_async_copy(sent, sent, grad_send).wait()
    pltpu.make_async_copy(others, others, norm_send).wait()
    pltpu.make_async_copy(sent, sent, gather_send).wait()
    pltpu.make_async_copy(gathered, gathered, gather_recv).wait()


def shards(grads, master, first_q, first_scale, second_q, second_scale):
    n = lax.axis_size("dp")
    blocks, width = grads.shape[1:]
    own = master.shape[0]
    vmem = pl.BlockSpec(memory_space=pltpu.VMEM)
    hbm = pl.BlockSpec(memory_space=pl.ANY)
    shape = jax.ShapeDtypeStruct
    outs = pl.pallas_call(
        functools.partial(step_kernel, n, blocks * width),
        out_shape=(
            shape((blocks, width), jnp.bfloat16),
            shape((own, width), jnp.float32),
            shape((own, width), jnp.bfloat16),
            shape((1, own), jnp.float32),
            shape((own, width), jnp.bfloat16),
            shape((1, own), jnp.float32),
        ),
        in_specs=[hbm] + [vmem] * 5,
        out_specs=[hbm] + [vmem] * 5,
        scratch_shapes=[
            pltpu.VMEM((blocks, width), jnp.bfloat16),
            pltpu.VMEM((n - 1, own, width), jnp.bfloat16),
            pltpu.VMEM((n, width), jnp.float32),
            pltpu.VMEM((own, width), jnp.bfloat16),
        ]
        + [pltpu.SemaphoreType.DMA] * 8,
        compiler_params=pltpu.CompilerParams(collective_id=0, has_side_effects=True),
    )(grads, master, first_q, first_scale.reshape(1, own), second_q, second_scale.reshape(1, own))
    weights, master_new, first_q_new, first_scale_new, second_q_new, second_scale_new = outs
    return (
        weights,
        master_new,
        first_q_new,
        first_scale_new.reshape(own),
        second_q_new,
        second_scale_new.reshape(own),
    )


def solution(mesh):
    placed = (P("dp", None, None), P("dp", None), P("dp", None), P("dp"), P("dp", None), P("dp"))
    return jax.shard_map(
        shards,
        mesh=mesh,
        in_specs=placed,
        out_specs=(P(), P("dp", None), P("dp", None), P("dp"), P("dp", None), P("dp")),
        check_vma=False,
    )
```

```python
import functools

import jax
import jax.numpy as jnp
from jax import lax
from jax.experimental import pallas as pl
from jax.experimental.pallas import tpu as pltpu
from jax.sharding import PartitionSpec as P

MESH = pl.DeviceIdType.MESH

beta_one = 0.9
beta_two = 0.95
learn_rate = 0.05
decay_rate = 0.1
adam_epsilon = 1e-08
clip_rms = 0.01
first_fix = 1.0 - 0.9**10
second_fix = 1.0 - 0.95**10


def column_of(row, count):
    down = lax.broadcasted_iota(jnp.int32, (count, count), 0)
    along = lax.broadcasted_iota(jnp.int32, (count, count), 1)
    spread = jnp.broadcast_to(row, (count, count))
    return jnp.sum(jnp.where(down == along, spread, 0.0), axis=1, keepdims=True)


def row_of(column, count):
    down = lax.broadcasted_iota(jnp.int32, (count, count), 0)
    along = lax.broadcasted_iota(jnp.int32, (count, count), 1)
    spread = jnp.broadcast_to(column, (count, count))
    return jnp.sum(jnp.where(down == along, spread, 0.0), axis=0, keepdims=True)


def step_kernel(
    n,
    entries,
    grads_ref,
    master_ref,
    first_q_ref,
    first_scale_ref,
    second_q_ref,
    second_scale_ref,
    weights_ref,
    master_new_ref,
    first_q_new_ref,
    first_scale_new_ref,
    second_q_new_ref,
    second_scale_new_ref,
    local,
    arrived,
    squares,
    mine,
    master,
    first_q,
    first_scale,
    second_q,
    second_scale,
    stage_sems,
    state_sems,
    grad_send,
    grad_recv,
    norm_send,
    norm_recv,
    gather_send,
    gather_recv,
):
    me = lax.axis_index("dp")
    own = master.shape[0]
    partners = [lax.rem(me + k, n) for k in range(1, n)]

    stage = pltpu.make_async_copy(grads_ref.at[0], local, stage_sems.at[0])
    stage.start()

    barrier = pltpu.get_barrier_semaphore()
    for to in partners:
        pl.semaphore_signal(barrier, inc=1, device_id=(to,), device_id_type=MESH)

    states = (
        (master_ref, master),
        (first_q_ref, first_q),
        (first_scale_ref, first_scale),
        (second_q_ref, second_q),
        (second_scale_ref, second_scale),
    )
    reads = [
        pltpu.make_async_copy(src, dst, state_sems.at[i]) for i, (src, dst) in enumerate(states)
    ]
    for read in reads:
        read.start()
    stage.wait()
    pl.semaphore_wait(barrier, n - 1)

    for k, to in enumerate(partners):
        pltpu.make_async_remote_copy(
            src_ref=local.at[pl.ds(pl.multiple_of(to * own, own), own)],
            dst_ref=arrived.at[k],
            send_sem=grad_send,
            recv_sem=grad_recv,
            device_id=(to,),
            device_id_type=MESH,
        ).start()

    for read in reads:
        read.wait()
    total = local[pl.ds(pl.multiple_of(me * own, own), own), :].astype(jnp.float32)
    first = beta_one * (first_q[...].astype(jnp.float32) * column_of(first_scale[...], own))
    second = beta_two * (second_q[...].astype(jnp.float32) * column_of(second_scale[...], own))
    kept = master[...] * (1.0 - learn_rate * decay_rate)
    pltpu.make_async_copy(arrived, arrived, grad_recv).wait()
    total = total + jnp.sum(arrived[...].astype(jnp.float32), axis=0)

    squares[pl.ds(n - 1, 1), :] = jnp.sum(total * total, axis=0, keepdims=True)
    for k, to in enumerate(partners):
        pltpu.make_async_remote_copy(
            src_ref=squares.at[pl.ds(n - 1, 1)],
            dst_ref=squares.at[pl.ds(k, 1)],
            send_sem=norm_send,
            recv_sem=norm_recv,
            device_id=(to,),
            device_id_type=MESH,
        ).start()

    others = squares.at[pl.ds(0, n - 1)]
    pltpu.make_async_copy(others, others, norm_recv).wait()
    norm = jnp.sqrt(jnp.sum(squares[...], keepdims=True))
    limit = clip_rms * jnp.sqrt(jnp.float32(entries))
    factor = jnp.minimum(1.0, limit / (norm + 1e-06))
    clipped = factor * total
    first_new = first + (1.0 - beta_one) * clipped
    second_new = second + (1.0 - beta_two) * clipped * clipped
    change = first_new / first_fix / (jnp.sqrt(second_new / second_fix) + adam_epsilon)
    master_new = kept - learn_rate * change
    mine[...] = master_new.astype(jnp.bfloat16)

    slot = weights_ref.at[pl.ds(pl.multiple_of(me * own, own), own)]
    for to in partners:
        pltpu.make_async_remote_copy(
            src_ref=mine,
            dst_ref=slot,
            send_sem=gather_send,
            recv_sem=gather_recv,
            device_id=(to,),
            device_id_type=MESH,
        ).start()
    keep = pltpu.make_async_copy(mine, slot, stage_sems.at[1])
    keep.start()

    first_top = jnp.max(jnp.abs(first_new), axis=1, keepdims=True) + 1e-08
    second_top = jnp.max(jnp.abs(second_new), axis=1, keepdims=True) + 1e-08
    master[...] = master_new
    first_q[...] = (first_new / first_top).astype(jnp.bfloat16)
    second_q[...] = (second_new / second_top).astype(jnp.bfloat16)
    first_scale[...] = row_of(first_top, own)
    second_scale[...] = row_of(second_top, own)
    results = (
        (master, master_new_ref),
        (first_q, first_q_new_ref),
        (first_scale, first_scale_new_ref),
        (second_q, second_q_new_ref),
        (second_scale, second_scale_new_ref),
    )
    writes = [
        pltpu.make_async_copy(src, dst, state_sems.at[i]) for i, (src, dst) in enumerate(results)
    ]
    for write in writes:
        write.start()

    sent = local.at[pl.ds(0, (n - 1) * own)]
    gathered = weights_ref.at[pl.ds(0, (n - 1) * own)]
    pltpu.make_async_copy(sent, sent, grad_send).wait()
    pltpu.make_async_copy(others, others, norm_send).wait()
    keep.wait()
    for write in writes:
        write.wait()
    pltpu.make_async_copy(sent, sent, gather_send).wait()
    pltpu.make_async_copy(gathered, gathered, gather_recv).wait()


def place_kernel(count, *refs):
    sems = refs[-1]
    copies = [
        pltpu.make_async_copy(refs[i], refs[count + i], sems.at[i]) for i in range(count)
    ]
    for copy in copies:
        copy.start()
    for copy in copies:
        copy.wait()


def shards(grads, master, first_q, first_scale, second_q, second_scale):
    n = lax.axis_size("dp")
    blocks, width = grads.shape[1:]
    own = master.shape[0]
    anywhere = pl.BlockSpec(memory_space=pl.ANY)
    shape = jax.ShapeDtypeStruct
    out_shape = (
        shape((blocks, width), jnp.bfloat16),
        shape((own, width), jnp.float32),
        shape((own, width), jnp.bfloat16),
        shape((1, own), jnp.float32),
        shape((own, width), jnp.bfloat16),
        shape((1, own), jnp.float32),
    )
    count = len(out_shape)
    outs = pl.pallas_call(
        functools.partial(step_kernel, n, blocks * width),
        out_shape=out_shape,
        in_specs=[anywhere] * 6,
        out_specs=[anywhere] * count,
        scratch_shapes=[
            pltpu.VMEM((blocks, width), jnp.bfloat16),
            pltpu.VMEM((n - 1, own, width), jnp.bfloat16),
            pltpu.VMEM((n, width), jnp.float32),
            pltpu.VMEM((own, width), jnp.bfloat16),
            pltpu.VMEM((own, width), jnp.float32),
            pltpu.VMEM((own, width), jnp.bfloat16),
            pltpu.VMEM((1, own), jnp.float32),
            pltpu.VMEM((own, width), jnp.bfloat16),
            pltpu.VMEM((1, own), jnp.float32),
            pltpu.SemaphoreType.DMA((2,)),
            pltpu.SemaphoreType.DMA((5,)),
        ]
        + [pltpu.SemaphoreType.DMA] * 6,
        compiler_params=pltpu.CompilerParams(collective_id=0, has_side_effects=True),
    )(grads, master, first_q, first_scale.reshape(1, own), second_q, second_scale.reshape(1, own))
    outs = pl.pallas_call(
        functools.partial(place_kernel, count),
        out_shape=out_shape,
        in_specs=[anywhere] * count,
        out_specs=[anywhere] * count,
        scratch_shapes=[pltpu.SemaphoreType.DMA((count,))],
    )(*outs)
    weights, master_new, first_q_new, first_scale_new, second_q_new, second_scale_new = outs
    return (
        weights,
        master_new,
        first_q_new,
        first_scale_new.reshape(own),
        second_q_new,
        second_scale_new.reshape(own),
    )


def solution(mesh):
    placed = (P("dp", None, None), P("dp", None), P("dp", None), P("dp"), P("dp", None), P("dp"))
    return jax.shard_map(
        shards,
        mesh=mesh,
        in_specs=placed,
        out_specs=(P(), P("dp", None), P("dp", None), P("dp"), P("dp", None), P("dp")),
        check_vma=False,
    )
```

```python
import functools

import jax
import jax.numpy as jnp
from jax import lax
from jax.experimental import pallas as pl
from jax.experimental.pallas import tpu as pltpu
from jax.sharding import PartitionSpec as P

MESH = pl.DeviceIdType.MESH

beta_one = 0.9
beta_two = 0.95
learn_rate = 0.05
decay_rate = 0.1
adam_epsilon = 1e-08
clip_rms = 0.01
first_fix = 1.0 - 0.9**10
second_fix = 1.0 - 0.95**10


def column_of(row, count):
    down = lax.broadcasted_iota(jnp.int32, (count, count), 0)
    along = lax.broadcasted_iota(jnp.int32, (count, count), 1)
    spread = jnp.broadcast_to(row, (count, count))
    return jnp.sum(jnp.where(down == along, spread, 0.0), axis=1, keepdims=True)


def row_of(column, count):
    down = lax.broadcasted_iota(jnp.int32, (count, count), 0)
    along = lax.broadcasted_iota(jnp.int32, (count, count), 1)
    spread = jnp.broadcast_to(column, (count, count))
    return jnp.sum(jnp.where(down == along, spread, 0.0), axis=0, keepdims=True)


def step_kernel(
    n,
    entries,
    grads_ref,
    master_ref,
    first_q_ref,
    first_scale_ref,
    second_q_ref,
    second_scale_ref,
    weights_ref,
    master_new_ref,
    first_q_new_ref,
    first_scale_new_ref,
    second_q_new_ref,
    second_scale_new_ref,
    local,
    arrived,
    squares,
    mine,
    master,
    first_q,
    first_scale,
    second_q,
    second_scale,
    stage_sems,
    state_sems,
    grad_send,
    grad_recv,
    norm_send,
    norm_recv,
    gather_send,
    gather_recv,
):
    me = lax.axis_index("dp")
    own = master.shape[0]
    partners = [lax.rem(me + k, n) for k in range(1, n)]

    stage = pltpu.make_async_copy(grads_ref.at[0], local, stage_sems.at[0])
    stage.start()

    barrier = pltpu.get_barrier_semaphore()
    for to in partners:
        pl.semaphore_signal(barrier, inc=1, device_id=(to,), device_id_type=MESH)

    states = (
        (master_ref, master),
        (first_q_ref, first_q),
        (first_scale_ref, first_scale),
        (second_q_ref, second_q),
        (second_scale_ref, second_scale),
    )
    reads = [
        pltpu.make_async_copy(src, dst, state_sems.at[i]) for i, (src, dst) in enumerate(states)
    ]
    for read in reads:
        read.start()
    stage.wait()
    pl.semaphore_wait(barrier, n - 1)

    for k, to in enumerate(partners):
        pltpu.make_async_remote_copy(
            src_ref=local.at[pl.ds(pl.multiple_of(to * own, own), own)],
            dst_ref=arrived.at[k],
            send_sem=grad_send,
            recv_sem=grad_recv,
            device_id=(to,),
            device_id_type=MESH,
        ).start()

    for read in reads:
        read.wait()
    total = local[pl.ds(pl.multiple_of(me * own, own), own), :].astype(jnp.float32)
    first = beta_one * (first_q[...].astype(jnp.float32) * column_of(first_scale[...], own))
    second = beta_two * (second_q[...].astype(jnp.float32) * column_of(second_scale[...], own))
    kept = master[...] * (1.0 - learn_rate * decay_rate)
    pltpu.make_async_copy(arrived, arrived, grad_recv).wait()
    total = total + jnp.sum(arrived[...].astype(jnp.float32), axis=0)

    squares[pl.ds(n - 1, 1), :] = jnp.sum(total * total, axis=0, keepdims=True)
    for k, to in enumerate(partners):
        pltpu.make_async_remote_copy(
            src_ref=squares.at[pl.ds(n - 1, 1)],
            dst_ref=squares.at[pl.ds(k, 1)],
            send_sem=norm_send,
            recv_sem=norm_recv,
            device_id=(to,),
            device_id_type=MESH,
        ).start()

    others = squares.at[pl.ds(0, n - 1)]
    pltpu.make_async_copy(others, others, norm_recv).wait()
    norm = jnp.sqrt(jnp.sum(squares[...], keepdims=True))
    limit = clip_rms * jnp.sqrt(jnp.float32(entries))
    factor = jnp.minimum(1.0, limit / (norm + 1e-06))
    clipped = factor * total
    first_new = first + (1.0 - beta_one) * clipped
    second_new = second + (1.0 - beta_two) * clipped * clipped
    change = first_new / first_fix / (jnp.sqrt(second_new / second_fix) + adam_epsilon)
    master_new = kept - learn_rate * change
    mine[...] = master_new.astype(jnp.bfloat16)

    slot = weights_ref.at[pl.ds(pl.multiple_of(me * own, own), own)]
    for to in partners:
        pltpu.make_async_remote_copy(
            src_ref=mine,
            dst_ref=slot,
            send_sem=gather_send,
            recv_sem=gather_recv,
            device_id=(to,),
            device_id_type=MESH,
        ).start()
    keep = pltpu.make_async_copy(mine, slot, stage_sems.at[1])
    keep.start()

    first_top = jnp.max(jnp.abs(first_new), axis=1, keepdims=True) + 1e-08
    second_top = jnp.max(jnp.abs(second_new), axis=1, keepdims=True) + 1e-08
    master_new_ref[...] = master_new
    first_q_new_ref[...] = (first_new / first_top).astype(jnp.bfloat16)
    second_q_new_ref[...] = (second_new / second_top).astype(jnp.bfloat16)
    first_scale_new_ref[...] = row_of(first_top, own)
    second_scale_new_ref[...] = row_of(second_top, own)

    sent = local.at[pl.ds(0, (n - 1) * own)]
    gathered = weights_ref.at[pl.ds(0, (n - 1) * own)]
    pltpu.make_async_copy(sent, sent, grad_send).wait()
    pltpu.make_async_copy(others, others, norm_send).wait()
    keep.wait()
    pltpu.make_async_copy(sent, sent, gather_send).wait()
    pltpu.make_async_copy(gathered, gathered, gather_recv).wait()


def place_kernel(count, *refs):
    sems = refs[-1]
    copies = [
        pltpu.make_async_copy(refs[i], refs[count + i], sems.at[i]) for i in range(count)
    ]
    for copy in copies:
        copy.start()
    for copy in copies:
        copy.wait()


def shards(grads, master, first_q, first_scale, second_q, second_scale):
    n = lax.axis_size("dp")
    blocks, width = grads.shape[1:]
    own = master.shape[0]
    anywhere = pl.BlockSpec(memory_space=pl.ANY)
    near = pl.BlockSpec(memory_space=pltpu.VMEM)
    shape = jax.ShapeDtypeStruct
    out_shape = (
        shape((blocks, width), jnp.bfloat16),
        shape((own, width), jnp.float32),
        shape((own, width), jnp.bfloat16),
        shape((1, own), jnp.float32),
        shape((own, width), jnp.bfloat16),
        shape((1, own), jnp.float32),
    )
    count = len(out_shape)
    outs = pl.pallas_call(
        functools.partial(step_kernel, n, blocks * width),
        out_shape=tuple(pltpu.VMEM(out.shape, out.dtype) for out in out_shape),
        in_specs=[anywhere] * 6,
        out_specs=[near] * count,
        scratch_shapes=[
            pltpu.VMEM((blocks, width), jnp.bfloat16),
            pltpu.VMEM((n - 1, own, width), jnp.bfloat16),
            pltpu.VMEM((n, width), jnp.float32),
            pltpu.VMEM((own, width), jnp.bfloat16),
            pltpu.VMEM((own, width), jnp.float32),
            pltpu.VMEM((own, width), jnp.bfloat16),
            pltpu.VMEM((1, own), jnp.float32),
            pltpu.VMEM((own, width), jnp.bfloat16),
            pltpu.VMEM((1, own), jnp.float32),
            pltpu.SemaphoreType.DMA((2,)),
            pltpu.SemaphoreType.DMA((5,)),
        ]
        + [pltpu.SemaphoreType.DMA] * 6,
        compiler_params=pltpu.CompilerParams(collective_id=0, has_side_effects=True),
    )(grads, master, first_q, first_scale.reshape(1, own), second_q, second_scale.reshape(1, own))
    outs = pl.pallas_call(
        functools.partial(place_kernel, count),
        out_shape=out_shape,
        in_specs=[near] * count,
        out_specs=[anywhere] * count,
        scratch_shapes=[pltpu.SemaphoreType.DMA((count,))],
    )(*outs)
    weights, master_new, first_q_new, first_scale_new, second_q_new, second_scale_new = outs
    return (
        weights,
        master_new,
        first_q_new,
        first_scale_new.reshape(own),
        second_q_new,
        second_scale_new.reshape(own),
    )


def solution(mesh):
    placed = (P("dp", None, None), P("dp", None), P("dp", None), P("dp"), P("dp", None), P("dp"))
    return jax.shard_map(
        shards,
        mesh=mesh,
        in_specs=placed,
        out_specs=(P(), P("dp", None), P("dp", None), P("dp"), P("dp", None), P("dp")),
        check_vma=False,
    )
```

```python
import functools

import jax
import jax.numpy as jnp
from jax import lax
from jax.experimental import pallas as pl
from jax.experimental.pallas import tpu as pltpu
from jax.sharding import PartitionSpec as P

MESH = pl.DeviceIdType.MESH

beta_one = 0.9
beta_two = 0.95
learn_rate = 0.05
decay_rate = 0.1
adam_epsilon = 1e-08
clip_rms = 0.01
first_fix = 1.0 - 0.9**10
second_fix = 1.0 - 0.95**10


def column_of(row, count):
    down = lax.broadcasted_iota(jnp.int32, (count, count), 0)
    along = lax.broadcasted_iota(jnp.int32, (count, count), 1)
    spread = jnp.broadcast_to(row, (count, count))
    return jnp.sum(jnp.where(down == along, spread, 0.0), axis=1, keepdims=True)


def row_of(column, count):
    down = lax.broadcasted_iota(jnp.int32, (count, count), 0)
    along = lax.broadcasted_iota(jnp.int32, (count, count), 1)
    spread = jnp.broadcast_to(column, (count, count))
    return jnp.sum(jnp.where(down == along, spread, 0.0), axis=0, keepdims=True)


def step_kernel(
    n,
    entries,
    grads_ref,
    master_ref,
    first_q_ref,
    first_scale_ref,
    second_q_ref,
    second_scale_ref,
    weights_ref,
    master_new_ref,
    first_q_new_ref,
    first_scale_new_ref,
    second_q_new_ref,
    second_scale_new_ref,
    local,
    arrived,
    squares,
    mine,
    master,
    first_q,
    first_scale,
    second_q,
    second_scale,
    stage_sems,
    state_sems,
    grad_send,
    grad_recv,
    norm_send,
    norm_recv,
    gather_send,
    gather_recv,
):
    me = lax.axis_index("dp")
    own = master.shape[0]
    partners = [lax.rem(me + k, n) for k in range(1, n)]

    stage = pltpu.make_async_copy(grads_ref.at[0], local, stage_sems.at[0])
    stage.start()

    barrier = pltpu.get_barrier_semaphore()
    for to in partners:
        pl.semaphore_signal(barrier, inc=1, device_id=(to,), device_id_type=MESH)

    states = (
        (master_ref, master),
        (first_q_ref, first_q),
        (first_scale_ref, first_scale),
        (second_q_ref, second_q),
        (second_scale_ref, second_scale),
    )
    reads = [
        pltpu.make_async_copy(src, dst, state_sems.at[i]) for i, (src, dst) in enumerate(states)
    ]
    for read in reads:
        read.start()
    stage.wait()
    pl.semaphore_wait(barrier, n - 1)

    for k, to in enumerate(partners):
        pltpu.make_async_remote_copy(
            src_ref=local.at[pl.ds(pl.multiple_of(to * own, own), own)],
            dst_ref=arrived.at[k],
            send_sem=grad_send,
            recv_sem=grad_recv,
            device_id=(to,),
            device_id_type=MESH,
        ).start()

    for read in reads:
        read.wait()
    total = local[pl.ds(pl.multiple_of(me * own, own), own), :].astype(jnp.float32)
    first = beta_one * (first_q[...].astype(jnp.float32) * column_of(first_scale[...], own))
    second = beta_two * (second_q[...].astype(jnp.float32) * column_of(second_scale[...], own))
    kept = master[...] * (1.0 - learn_rate * decay_rate)
    pltpu.make_async_copy(arrived, arrived, grad_recv).wait()
    total = total + jnp.sum(arrived[...].astype(jnp.float32), axis=0)

    squares[pl.ds(n - 1, 1), :] = jnp.sum(total * total, axis=0, keepdims=True)
    for k, to in enumerate(partners):
        pltpu.make_async_remote_copy(
            src_ref=squares.at[pl.ds(n - 1, 1)],
            dst_ref=squares.at[pl.ds(k, 1)],
            send_sem=norm_send,
            recv_sem=norm_recv,
            device_id=(to,),
            device_id_type=MESH,
        ).start()

    others = squares.at[pl.ds(0, n - 1)]
    pltpu.make_async_copy(others, others, norm_recv).wait()
    norm = jnp.sqrt(jnp.sum(squares[...], keepdims=True))
    limit = clip_rms * jnp.sqrt(jnp.float32(entries))
    factor = jnp.minimum(1.0, limit / (norm + 1e-06))
    clipped = factor * total
    first_new = first + (1.0 - beta_one) * clipped
    second_new = second + (1.0 - beta_two) * clipped * clipped
    change = first_new / first_fix / (jnp.sqrt(second_new / second_fix) + adam_epsilon)
    master_new = kept - learn_rate * change
    mine[...] = master_new.astype(jnp.bfloat16)

    slot = weights_ref.at[pl.ds(pl.multiple_of(me * own, own), own)]
    for to in partners:
        pltpu.make_async_remote_copy(
            src_ref=mine,
            dst_ref=slot,
            send_sem=gather_send,
            recv_sem=gather_recv,
            device_id=(to,),
            device_id_type=MESH,
        ).start()
    keep = pltpu.make_async_copy(mine, slot, stage_sems.at[1])
    keep.start()

    first_top = jnp.max(jnp.abs(first_new), axis=1, keepdims=True) + 1e-08
    second_top = jnp.max(jnp.abs(second_new), axis=1, keepdims=True) + 1e-08
    master_new_ref[...] = master_new
    first_q_new_ref[...] = (first_new / first_top).astype(jnp.bfloat16)
    second_q_new_ref[...] = (second_new / second_top).astype(jnp.bfloat16)
    first_scale_new_ref[...] = row_of(first_top, own)
    second_scale_new_ref[...] = row_of(second_top, own)

    sent = local.at[pl.ds(0, (n - 1) * own)]
    gathered = weights_ref.at[pl.ds(0, (n - 1) * own)]
    pltpu.make_async_copy(sent, sent, grad_send).wait()
    pltpu.make_async_copy(others, others, norm_send).wait()
    keep.wait()
    pltpu.make_async_copy(sent, sent, gather_send).wait()
    pltpu.make_async_copy(gathered, gathered, gather_recv).wait()


def place_kernel(count, *refs):
    sems = refs[-1]
    copies = [
        pltpu.make_async_copy(refs[i], refs[count + i], sems.at[i]) for i in range(count)
    ]
    for copy in copies:
        copy.start()
    for copy in copies:
        copy.wait()


def shards(grads, master, first_q, first_scale, second_q, second_scale):
    n = lax.axis_size("dp")
    blocks, width = grads.shape[1:]
    own = master.shape[0]
    anywhere = pl.BlockSpec(memory_space=pl.ANY)
    near = pl.BlockSpec(memory_space=pltpu.VMEM)
    shape = jax.ShapeDtypeStruct
    out_shape = (
        shape((blocks, width), jnp.bfloat16),
        shape((own, width), jnp.float32),
        shape((own, width), jnp.bfloat16),
        shape((1, own), jnp.float32),
        shape((own, width), jnp.bfloat16),
        shape((1, own), jnp.float32),
    )
    count = len(out_shape)
    outs = pl.pallas_call(
        functools.partial(step_kernel, n, blocks * width),
        out_shape=tuple(pltpu.VMEM(out.shape, out.dtype) for out in out_shape),
        in_specs=[anywhere] * 6,
        out_specs=[near] * count,
        scratch_shapes=[
            pltpu.VMEM((blocks, width), jnp.bfloat16),
            pltpu.VMEM((n - 1, own, width), jnp.bfloat16),
            pltpu.VMEM((n, width), jnp.float32),
            pltpu.VMEM((own, width), jnp.bfloat16),
            pltpu.VMEM((own, width), jnp.float32),
            pltpu.VMEM((own, width), jnp.bfloat16),
            pltpu.VMEM((1, own), jnp.float32),
            pltpu.VMEM((own, width), jnp.bfloat16),
            pltpu.VMEM((1, own), jnp.float32),
            pltpu.SemaphoreType.DMA((2,)),
            pltpu.SemaphoreType.DMA((5,)),
        ]
        + [pltpu.SemaphoreType.DMA] * 6,
        compiler_params=pltpu.CompilerParams(collective_id=0, has_side_effects=True),
    )(grads, master, first_q, first_scale.reshape(1, own), second_q, second_scale.reshape(1, own))
    outs = pl.pallas_call(
        functools.partial(place_kernel, count),
        out_shape=out_shape,
        in_specs=[near] * count,
        out_specs=[anywhere] * count,
        scratch_shapes=[pltpu.SemaphoreType.DMA((count,))],
    )(*[pltpu.with_memory_space_constraint(out, pltpu.VMEM) for out in outs])
    weights, master_new, first_q_new, first_scale_new, second_q_new, second_scale_new = outs
    return (
        weights,
        master_new,
        first_q_new,
        first_scale_new.reshape(own),
        second_q_new,
        second_scale_new.reshape(own),
    )


def solution(mesh):
    placed = (P("dp", None, None), P("dp", None), P("dp", None), P("dp"), P("dp", None), P("dp"))
    return jax.shard_map(
        shards,
        mesh=mesh,
        in_specs=placed,
        out_specs=(P(), P("dp", None), P("dp", None), P("dp"), P("dp", None), P("dp")),
        check_vma=False,
    )
```

```python
import functools

import jax
import jax.numpy as jnp
from jax import lax
from jax.experimental import pallas as pl
from jax.experimental.pallas import tpu as pltpu
from jax.sharding import PartitionSpec as P

MESH = pl.DeviceIdType.MESH

beta_one = 0.9
beta_two = 0.95
learn_rate = 0.05
decay_rate = 0.1
adam_epsilon = 1e-08
clip_rms = 0.01
first_fix = 1.0 - 0.9**10
second_fix = 1.0 - 0.95**10


def column_of(row, count):
    down = lax.broadcasted_iota(jnp.int32, (count, count), 0)
    along = lax.broadcasted_iota(jnp.int32, (count, count), 1)
    spread = jnp.broadcast_to(row, (count, count))
    return jnp.sum(jnp.where(down == along, spread, 0.0), axis=1, keepdims=True)


def row_of(column, count):
    down = lax.broadcasted_iota(jnp.int32, (count, count), 0)
    along = lax.broadcasted_iota(jnp.int32, (count, count), 1)
    spread = jnp.broadcast_to(column, (count, count))
    return jnp.sum(jnp.where(down == along, spread, 0.0), axis=0, keepdims=True)


def push(src, dst, send_sem, recv_sem, to):
    pltpu.make_async_remote_copy(
        src_ref=src,
        dst_ref=dst,
        send_sem=send_sem,
        recv_sem=recv_sem,
        device_id=(to,),
        device_id_type=MESH,
    ).start()


def drain(ref, sem):
    pltpu.make_async_copy(ref, ref, sem).wait()


def step_kernel(
    outer,
    inner,
    entries,
    grads_ref,
    master_ref,
    first_q_ref,
    first_scale_ref,
    second_q_ref,
    second_scale_ref,
    weights_ref,
    master_new_ref,
    first_q_new_ref,
    first_scale_new_ref,
    second_q_new_ref,
    second_scale_new_ref,
    local,
    near_grads,
    partial,
    far_grads,
    near_squares,
    far_squares,
    master,
    first_q,
    first_scale,
    second_q,
    second_scale,
    stage_sem,
    state_sems,
    send_sems,
    recv_sems,
):
    me = lax.axis_index("dp")
    own = master.shape[0]
    group = lax.div(me, inner)
    place = lax.rem(me, inner)
    near_places = [lax.rem(place + k, inner) for k in range(1, inner)]
    near = [group * inner + p for p in near_places]
    far_groups = [lax.rem(group + k, outer) for k in range(1, outer)]
    far = [g * inner + place for g in far_groups]

    stage = pltpu.make_async_copy(grads_ref, local, stage_sem)
    stage.start()
    barrier = pltpu.get_barrier_semaphore()
    for to in near + far:
        pl.semaphore_signal(barrier, inc=1, device_id=(to,), device_id_type=MESH)

    states = (
        (master_ref, master),
        (first_q_ref, first_q),
        (first_scale_ref, first_scale),
        (second_q_ref, second_q),
        (second_scale_ref, second_scale),
    )
    reads = [
        pltpu.make_async_copy(src, dst, state_sems.at[i]) for i, (src, dst) in enumerate(states)
    ]
    for read in reads:
        read.start()
    stage.wait()
    pl.semaphore_wait(barrier, inner + outer - 2)

    for k, (p, to) in enumerate(zip(near_places, near)):
        push(local.at[:, p], near_grads.at[k], send_sems.at[0], recv_sems.at[0], to)
    for read in reads:
        read.wait()
    first = beta_one * (first_q[...].astype(jnp.float32) * column_of(first_scale[...], own))
    second = beta_two * (second_q[...].astype(jnp.float32) * column_of(second_scale[...], own))
    kept = master[...] * (1.0 - learn_rate * decay_rate)
    drain(near_grads, recv_sems.at[0])
    sums = local[:, place].astype(jnp.float32)
    partial[...] = sums + jnp.sum(near_grads[...].astype(jnp.float32), axis=0)

    for k, (g, to) in enumerate(zip(far_groups, far)):
        push(partial.at[g], far_grads.at[k], send_sems.at[1], recv_sems.at[1], to)
    drain(far_grads, recv_sems.at[1])
    total = partial[group] + jnp.sum(far_grads[...], axis=0)

    far_squares[pl.ds(outer - 1, 1), :] = jnp.sum(total * total, axis=0, keepdims=True)
    for k, to in enumerate(far):
        push(
            far_squares.at[pl.ds(outer - 1, 1)],
            far_squares.at[pl.ds(k, 1)],
            send_sems.at[2],
            recv_sems.at[2],
            to,
        )
    far_rows = far_squares.at[pl.ds(0, outer - 1)]
    drain(far_rows, recv_sems.at[2])
    near_squares[pl.ds(inner - 1, 1), :] = jnp.sum(far_squares[...], axis=0, keepdims=True)
    for k, to in enumerate(near):
        push(
            near_squares.at[pl.ds(inner - 1, 1)],
            near_squares.at[pl.ds(k, 1)],
            send_sems.at[3],
            recv_sems.at[3],
            to,
        )
    near_rows = near_squares.at[pl.ds(0, inner - 1)]
    drain(near_rows, recv_sems.at[3])
    norm = jnp.sqrt(jnp.sum(near_squares[...], keepdims=True))
    limit = clip_rms * jnp.sqrt(jnp.float32(entries))
    factor = jnp.minimum(1.0, limit / (norm + 1e-06))
    clipped = factor * total
    first_new = first + (1.0 - beta_one) * clipped
    second_new = second + (1.0 - beta_two) * clipped * clipped
    change = first_new / first_fix / (jnp.sqrt(second_new / second_fix) + adam_epsilon)
    master_new = kept - learn_rate * change
    weights_ref[group, place] = master_new.astype(jnp.bfloat16)

    slot = weights_ref.at[group, place]
    for to in far:
        push(slot, slot, send_sems.at[4], recv_sems.at[4], to)

    first_top = jnp.max(jnp.abs(first_new), axis=1, keepdims=True) + 1e-08
    second_top = jnp.max(jnp.abs(second_new), axis=1, keepdims=True) + 1e-08
    master_new_ref[...] = master_new
    first_q_new_ref[...] = (first_new / first_top).astype(jnp.bfloat16)
    second_q_new_ref[...] = (second_new / second_top).astype(jnp.bfloat16)
    first_scale_new_ref[...] = row_of(first_top, own)
    second_scale_new_ref[...] = row_of(second_top, own)

    far_weights = weights_ref.at[pl.ds(0, outer - 1), 0]
    drain(far_weights, recv_sems.at[4])
    column = weights_ref.at[:, place]
    for to in near:
        push(column, column, send_sems.at[5], recv_sems.at[5], to)

    drain(near_grads, send_sems.at[0])
    drain(far_grads, send_sems.at[1])
    drain(far_rows, send_sems.at[2])
    drain(near_rows, send_sems.at[3])
    drain(far_weights, send_sems.at[4])
    near_weights = weights_ref.at[:, pl.ds(0, inner - 1)]
    drain(near_weights, send_sems.at[5])
    drain(near_weights, recv_sems.at[5])


def place_kernel(count, *refs):
    sems = refs[-1]
    copies = [
        pltpu.make_async_copy(refs[i], refs[count + i], sems.at[i]) for i in range(count)
    ]
    for copy in copies:
        copy.start()
    for copy in copies:
        copy.wait()


def shards(grads, master, first_q, first_scale, second_q, second_scale):
    n = lax.axis_size("dp")
    blocks, width = grads.shape[1:]
    own = master.shape[0]
    inner = 1
    while inner * inner < n:
        inner *= 2
    outer = n // inner
    anywhere = pl.BlockSpec(memory_space=pl.ANY)
    near = pl.BlockSpec(memory_space=pltpu.VMEM)
    shape = jax.ShapeDtypeStruct
    out_shape = (
        shape((outer, inner, own, width), jnp.bfloat16),
        shape((own, width), jnp.float32),
        shape((own, width), jnp.bfloat16),
        shape((1, own), jnp.float32),
        shape((own, width), jnp.bfloat16),
        shape((1, own), jnp.float32),
    )
    count = len(out_shape)
    outs = pl.pallas_call(
        functools.partial(step_kernel, outer, inner, blocks * width),
        out_shape=tuple(pltpu.VMEM(out.shape, out.dtype) for out in out_shape),
        in_specs=[anywhere] * 6,
        out_specs=[near] * count,
        scratch_shapes=[
            pltpu.VMEM((outer, inner, own, width), jnp.bfloat16),
            pltpu.VMEM((inner - 1, outer, own, width), jnp.bfloat16),
            pltpu.VMEM((outer, own, width), jnp.float32),
            pltpu.VMEM((outer - 1, own, width), jnp.float32),
            pltpu.VMEM((inner, width), jnp.float32),
            pltpu.VMEM((outer, width), jnp.float32),
            pltpu.VMEM((own, width), jnp.float32),
            pltpu.VMEM((own, width), jnp.bfloat16),
            pltpu.VMEM((1, own), jnp.float32),
            pltpu.VMEM((own, width), jnp.bfloat16),
            pltpu.VMEM((1, own), jnp.float32),
            pltpu.SemaphoreType.DMA,
            pltpu.SemaphoreType.DMA((5,)),
            pltpu.SemaphoreType.DMA((6,)),
            pltpu.SemaphoreType.DMA((6,)),
        ],
        compiler_params=pltpu.CompilerParams(collective_id=0, has_side_effects=True),
    )(grads.reshape(outer, inner, own, width), master, first_q, first_scale.reshape(1, own), second_q, second_scale.reshape(1, own))
    outs = pl.pallas_call(
        functools.partial(place_kernel, count),
        out_shape=out_shape,
        in_specs=[near] * count,
        out_specs=[anywhere] * count,
        scratch_shapes=[pltpu.SemaphoreType.DMA((count,))],
    )(*[pltpu.with_memory_space_constraint(out, pltpu.VMEM) for out in outs])
    weights, master_new, first_q_new, first_scale_new, second_q_new, second_scale_new = outs
    return (
        weights.reshape(blocks, width),
        master_new,
        first_q_new,
        first_scale_new.reshape(own),
        second_q_new,
        second_scale_new.reshape(own),
    )


def solution(mesh):
    placed = (P("dp", None, None), P("dp", None), P("dp", None), P("dp"), P("dp", None), P("dp"))
    return jax.shard_map(
        shards,
        mesh=mesh,
        in_specs=placed,
        out_specs=(P(), P("dp", None), P("dp", None), P("dp"), P("dp", None), P("dp")),
        check_vma=False,
    )
```

```python
import functools

import jax
import jax.numpy as jnp
from jax import lax
from jax.experimental import pallas as pl
from jax.experimental.pallas import tpu as pltpu
from jax.sharding import PartitionSpec as P

MESH = pl.DeviceIdType.MESH

beta_one = 0.9
beta_two = 0.95
learn_rate = 0.05
decay_rate = 0.1
adam_epsilon = 1e-08
clip_rms = 0.01
first_fix = 1.0 - 0.9**10
second_fix = 1.0 - 0.95**10


def column_of(row, count):
    down = lax.broadcasted_iota(jnp.int32, (count, count), 0)
    along = lax.broadcasted_iota(jnp.int32, (count, count), 1)
    spread = jnp.broadcast_to(row, (count, count))
    return jnp.sum(jnp.where(down == along, spread, 0.0), axis=1, keepdims=True)


def row_of(column, count):
    down = lax.broadcasted_iota(jnp.int32, (count, count), 0)
    along = lax.broadcasted_iota(jnp.int32, (count, count), 1)
    spread = jnp.broadcast_to(column, (count, count))
    return jnp.sum(jnp.where(down == along, spread, 0.0), axis=0, keepdims=True)


def step_kernel(
    n,
    entries,
    grads_ref,
    master_ref,
    first_q_ref,
    first_scale_ref,
    second_q_ref,
    second_scale_ref,
    weights_ref,
    master_new_ref,
    first_q_new_ref,
    first_scale_new_ref,
    second_q_new_ref,
    second_scale_new_ref,
    local,
    arrived,
    squares,
    mine,
    master,
    first_q,
    first_scale,
    second_q,
    second_scale,
    stage_sems,
    state_sems,
    grad_send,
    grad_recv,
    norm_send,
    norm_recv,
    gather_send,
    gather_recv,
):
    me = lax.axis_index("dp")
    own = master.shape[0]
    order = sorted(range(1, n), key=lambda k: abs(2 * k - n))
    partners = [(k - 1, lax.rem(me + k, n)) for k in order]

    stage = pltpu.make_async_copy(grads_ref.at[0], local, stage_sems.at[0])
    stage.start()

    barrier = pltpu.get_barrier_semaphore()
    for _, to in partners:
        pl.semaphore_signal(barrier, inc=1, device_id=(to,), device_id_type=MESH)

    states = (
        (master_ref, master),
        (first_q_ref, first_q),
        (first_scale_ref, first_scale),
        (second_q_ref, second_q),
        (second_scale_ref, second_scale),
    )
    reads = [
        pltpu.make_async_copy(src, dst, state_sems.at[i]) for i, (src, dst) in enumerate(states)
    ]
    for read in reads:
        read.start()
    stage.wait()
    pl.semaphore_wait(barrier, n - 1)

    for k, to in partners:
        pltpu.make_async_remote_copy(
            src_ref=local.at[pl.ds(pl.multiple_of(to * own, own), own)],
            dst_ref=arrived.at[k],
            send_sem=grad_send,
            recv_sem=grad_recv,
            device_id=(to,),
            device_id_type=MESH,
        ).start()

    for read in reads:
        read.wait()
    total = local[pl.ds(pl.multiple_of(me * own, own), own), :].astype(jnp.float32)
    first = beta_one * (first_q[...].astype(jnp.float32) * column_of(first_scale[...], own))
    second = beta_two * (second_q[...].astype(jnp.float32) * column_of(second_scale[...], own))
    kept = master[...] * (1.0 - learn_rate * decay_rate)
    pltpu.make_async_copy(arrived, arrived, grad_recv).wait()
    total = total + jnp.sum(arrived[...].astype(jnp.float32), axis=0)

    squares[pl.ds(n - 1, 1), :] = jnp.sum(total * total, axis=0, keepdims=True)
    for k, to in partners:
        pltpu.make_async_remote_copy(
            src_ref=squares.at[pl.ds(n - 1, 1)],
            dst_ref=squares.at[pl.ds(k, 1)],
            send_sem=norm_send,
            recv_sem=norm_recv,
            device_id=(to,),
            device_id_type=MESH,
        ).start()

    others = squares.at[pl.ds(0, n - 1)]
    pltpu.make_async_copy(others, others, norm_recv).wait()
    norm = jnp.sqrt(jnp.sum(squares[...], keepdims=True))
    limit = clip_rms * jnp.sqrt(jnp.float32(entries))
    factor = jnp.minimum(1.0, limit / (norm + 1e-06))
    clipped = factor * total
    first_new = first + (1.0 - beta_one) * clipped
    second_new = second + (1.0 - beta_two) * clipped * clipped
    change = first_new / first_fix / (jnp.sqrt(second_new / second_fix) + adam_epsilon)
    master_new = kept - learn_rate * change
    mine[...] = master_new.astype(jnp.bfloat16)

    slot = weights_ref.at[pl.ds(pl.multiple_of(me * own, own), own)]
    for _, to in partners:
        pltpu.make_async_remote_copy(
            src_ref=mine,
            dst_ref=slot,
            send_sem=gather_send,
            recv_sem=gather_recv,
            device_id=(to,),
            device_id_type=MESH,
        ).start()
    keep = pltpu.make_async_copy(mine, slot, stage_sems.at[1])
    keep.start()

    first_top = jnp.max(jnp.abs(first_new), axis=1, keepdims=True) + 1e-08
    second_top = jnp.max(jnp.abs(second_new), axis=1, keepdims=True) + 1e-08
    master_new_ref[...] = master_new
    first_q_new_ref[...] = (first_new / first_top).astype(jnp.bfloat16)
    second_q_new_ref[...] = (second_new / second_top).astype(jnp.bfloat16)
    first_scale_new_ref[...] = row_of(first_top, own)
    second_scale_new_ref[...] = row_of(second_top, own)

    sent = local.at[pl.ds(0, (n - 1) * own)]
    gathered = weights_ref.at[pl.ds(0, (n - 1) * own)]
    pltpu.make_async_copy(sent, sent, grad_send).wait()
    pltpu.make_async_copy(others, others, norm_send).wait()
    keep.wait()
    pltpu.make_async_copy(sent, sent, gather_send).wait()
    pltpu.make_async_copy(gathered, gathered, gather_recv).wait()


def place_kernel(count, *refs):
    sems = refs[-1]
    copies = [
        pltpu.make_async_copy(refs[i], refs[count + i], sems.at[i]) for i in range(count)
    ]
    for copy in copies:
        copy.start()
    for copy in copies:
        copy.wait()


def shards(grads, master, first_q, first_scale, second_q, second_scale):
    n = lax.axis_size("dp")
    blocks, width = grads.shape[1:]
    own = master.shape[0]
    anywhere = pl.BlockSpec(memory_space=pl.ANY)
    near = pl.BlockSpec(memory_space=pltpu.VMEM)
    shape = jax.ShapeDtypeStruct
    out_shape = (
        shape((blocks, width), jnp.bfloat16),
        shape((own, width), jnp.float32),
        shape((own, width), jnp.bfloat16),
        shape((1, own), jnp.float32),
        shape((own, width), jnp.bfloat16),
        shape((1, own), jnp.float32),
    )
    count = len(out_shape)
    outs = pl.pallas_call(
        functools.partial(step_kernel, n, blocks * width),
        out_shape=tuple(pltpu.VMEM(out.shape, out.dtype) for out in out_shape),
        in_specs=[anywhere] * 6,
        out_specs=[near] * count,
        scratch_shapes=[
            pltpu.VMEM((blocks, width), jnp.bfloat16),
            pltpu.VMEM((n - 1, own, width), jnp.bfloat16),
            pltpu.VMEM((n, width), jnp.float32),
            pltpu.VMEM((own, width), jnp.bfloat16),
            pltpu.VMEM((own, width), jnp.float32),
            pltpu.VMEM((own, width), jnp.bfloat16),
            pltpu.VMEM((1, own), jnp.float32),
            pltpu.VMEM((own, width), jnp.bfloat16),
            pltpu.VMEM((1, own), jnp.float32),
            pltpu.SemaphoreType.DMA((2,)),
            pltpu.SemaphoreType.DMA((5,)),
        ]
        + [pltpu.SemaphoreType.DMA] * 6,
        compiler_params=pltpu.CompilerParams(collective_id=0, has_side_effects=True),
    )(grads, master, first_q, first_scale.reshape(1, own), second_q, second_scale.reshape(1, own))
    outs = pl.pallas_call(
        functools.partial(place_kernel, count),
        out_shape=out_shape,
        in_specs=[near] * count,
        out_specs=[anywhere] * count,
        scratch_shapes=[pltpu.SemaphoreType.DMA((count,))],
    )(*[pltpu.with_memory_space_constraint(out, pltpu.VMEM) for out in outs])
    weights, master_new, first_q_new, first_scale_new, second_q_new, second_scale_new = outs
    return (
        weights,
        master_new,
        first_q_new,
        first_scale_new.reshape(own),
        second_q_new,
        second_scale_new.reshape(own),
    )


def solution(mesh):
    placed = (P("dp", None, None), P("dp", None), P("dp", None), P("dp"), P("dp", None), P("dp"))
    return jax.shard_map(
        shards,
        mesh=mesh,
        in_specs=placed,
        out_specs=(P(), P("dp", None), P("dp", None), P("dp"), P("dp", None), P("dp")),
        check_vma=False,
    )
```

```python
import functools

import jax
import jax.numpy as jnp
from jax import lax
from jax.experimental import pallas as pl
from jax.experimental.pallas import tpu as pltpu
from jax.sharding import PartitionSpec as P

MESH = pl.DeviceIdType.MESH

beta_one = 0.9
beta_two = 0.95
learn_rate = 0.05
decay_rate = 0.1
adam_epsilon = 1e-08
clip_rms = 0.01
first_fix = 1.0 - 0.9**10
second_fix = 1.0 - 0.95**10


def column_of(row, count):
    down = lax.broadcasted_iota(jnp.int32, (count, count), 0)
    along = lax.broadcasted_iota(jnp.int32, (count, count), 1)
    spread = jnp.broadcast_to(row, (count, count))
    return jnp.sum(jnp.where(down == along, spread, 0.0), axis=1, keepdims=True)


def row_of(column, count):
    down = lax.broadcasted_iota(jnp.int32, (count, count), 0)
    along = lax.broadcasted_iota(jnp.int32, (count, count), 1)
    spread = jnp.broadcast_to(column, (count, count))
    return jnp.sum(jnp.where(down == along, spread, 0.0), axis=0, keepdims=True)


def step_kernel(
    n,
    entries,
    grads_ref,
    master_ref,
    first_q_ref,
    first_scale_ref,
    second_q_ref,
    second_scale_ref,
    weights_ref,
    master_new_ref,
    first_q_new_ref,
    first_scale_new_ref,
    second_q_new_ref,
    second_scale_new_ref,
    local,
    arrived,
    squares,
    mine,
    master,
    first_q,
    first_scale,
    second_q,
    second_scale,
    stage_sems,
    state_sems,
    grad_send,
    grad_recv,
    norm_send,
    norm_recv,
    gather_send,
    gather_recv,
):
    me = lax.axis_index("dp")
    own = master.shape[0]
    order = sorted(range(1, n), key=lambda k: -abs(2 * k - n))
    partners = [(k - 1, lax.rem(me + k, n)) for k in order]

    stage = pltpu.make_async_copy(grads_ref.at[0], local, stage_sems.at[0])
    stage.start()

    barrier = pltpu.get_barrier_semaphore()
    for _, to in partners:
        pl.semaphore_signal(barrier, inc=1, device_id=(to,), device_id_type=MESH)

    states = (
        (master_ref, master),
        (first_q_ref, first_q),
        (first_scale_ref, first_scale),
        (second_q_ref, second_q),
        (second_scale_ref, second_scale),
    )
    reads = [
        pltpu.make_async_copy(src, dst, state_sems.at[i]) for i, (src, dst) in enumerate(states)
    ]
    for read in reads:
        read.start()
    stage.wait()
    pl.semaphore_wait(barrier, n - 1)

    for k, to in partners:
        pltpu.make_async_remote_copy(
            src_ref=local.at[pl.ds(pl.multiple_of(to * own, own), own)],
            dst_ref=arrived.at[k],
            send_sem=grad_send,
            recv_sem=grad_recv,
            device_id=(to,),
            device_id_type=MESH,
        ).start()

    for read in reads:
        read.wait()
    total = local[pl.ds(pl.multiple_of(me * own, own), own), :].astype(jnp.float32)
    first = beta_one * (first_q[...].astype(jnp.float32) * column_of(first_scale[...], own))
    second = beta_two * (second_q[...].astype(jnp.float32) * column_of(second_scale[...], own))
    kept = master[...] * (1.0 - learn_rate * decay_rate)
    pltpu.make_async_copy(arrived, arrived, grad_recv).wait()
    total = total + jnp.sum(arrived[...].astype(jnp.float32), axis=0)

    squares[pl.ds(n - 1, 1), :] = jnp.sum(total * total, axis=0, keepdims=True)
    for k, to in partners:
        pltpu.make_async_remote_copy(
            src_ref=squares.at[pl.ds(n - 1, 1)],
            dst_ref=squares.at[pl.ds(k, 1)],
            send_sem=norm_send,
            recv_sem=norm_recv,
            device_id=(to,),
            device_id_type=MESH,
        ).start()

    others = squares.at[pl.ds(0, n - 1)]
    pltpu.make_async_copy(others, others, norm_recv).wait()
    norm = jnp.sqrt(jnp.sum(squares[...], keepdims=True))
    limit = clip_rms * jnp.sqrt(jnp.float32(entries))
    factor = jnp.minimum(1.0, limit / (norm + 1e-06))
    clipped = factor * total
    first_new = first + (1.0 - beta_one) * clipped
    second_new = second + (1.0 - beta_two) * clipped * clipped
    change = first_new / first_fix / (jnp.sqrt(second_new / second_fix) + adam_epsilon)
    master_new = kept - learn_rate * change
    mine[...] = master_new.astype(jnp.bfloat16)

    slot = weights_ref.at[pl.ds(pl.multiple_of(me * own, own), own)]
    for _, to in partners:
        pltpu.make_async_remote_copy(
            src_ref=mine,
            dst_ref=slot,
            send_sem=gather_send,
            recv_sem=gather_recv,
            device_id=(to,),
            device_id_type=MESH,
        ).start()
    keep = pltpu.make_async_copy(mine, slot, stage_sems.at[1])
    keep.start()

    first_top = jnp.max(jnp.abs(first_new), axis=1, keepdims=True) + 1e-08
    second_top = jnp.max(jnp.abs(second_new), axis=1, keepdims=True) + 1e-08
    master_new_ref[...] = master_new
    first_q_new_ref[...] = (first_new / first_top).astype(jnp.bfloat16)
    second_q_new_ref[...] = (second_new / second_top).astype(jnp.bfloat16)
    first_scale_new_ref[...] = row_of(first_top, own)
    second_scale_new_ref[...] = row_of(second_top, own)

    sent = local.at[pl.ds(0, (n - 1) * own)]
    gathered = weights_ref.at[pl.ds(0, (n - 1) * own)]
    pltpu.make_async_copy(sent, sent, grad_send).wait()
    pltpu.make_async_copy(others, others, norm_send).wait()
    keep.wait()
    pltpu.make_async_copy(sent, sent, gather_send).wait()
    pltpu.make_async_copy(gathered, gathered, gather_recv).wait()


def place_kernel(count, *refs):
    sems = refs[-1]
    copies = [
        pltpu.make_async_copy(refs[i], refs[count + i], sems.at[i]) for i in range(count)
    ]
    for copy in copies:
        copy.start()
    for copy in copies:
        copy.wait()


def shards(grads, master, first_q, first_scale, second_q, second_scale):
    n = lax.axis_size("dp")
    blocks, width = grads.shape[1:]
    own = master.shape[0]
    anywhere = pl.BlockSpec(memory_space=pl.ANY)
    near = pl.BlockSpec(memory_space=pltpu.VMEM)
    shape = jax.ShapeDtypeStruct
    out_shape = (
        shape((blocks, width), jnp.bfloat16),
        shape((own, width), jnp.float32),
        shape((own, width), jnp.bfloat16),
        shape((1, own), jnp.float32),
        shape((own, width), jnp.bfloat16),
        shape((1, own), jnp.float32),
    )
    count = len(out_shape)
    outs = pl.pallas_call(
        functools.partial(step_kernel, n, blocks * width),
        out_shape=tuple(pltpu.VMEM(out.shape, out.dtype) for out in out_shape),
        in_specs=[anywhere] * 6,
        out_specs=[near] * count,
        scratch_shapes=[
            pltpu.VMEM((blocks, width), jnp.bfloat16),
            pltpu.VMEM((n - 1, own, width), jnp.bfloat16),
            pltpu.VMEM((n, width), jnp.float32),
            pltpu.VMEM((own, width), jnp.bfloat16),
            pltpu.VMEM((own, width), jnp.float32),
            pltpu.VMEM((own, width), jnp.bfloat16),
            pltpu.VMEM((1, own), jnp.float32),
            pltpu.VMEM((own, width), jnp.bfloat16),
            pltpu.VMEM((1, own), jnp.float32),
            pltpu.SemaphoreType.DMA((2,)),
            pltpu.SemaphoreType.DMA((5,)),
        ]
        + [pltpu.SemaphoreType.DMA] * 6,
        compiler_params=pltpu.CompilerParams(collective_id=0, has_side_effects=True),
    )(grads, master, first_q, first_scale.reshape(1, own), second_q, second_scale.reshape(1, own))
    outs = pl.pallas_call(
        functools.partial(place_kernel, count),
        out_shape=out_shape,
        in_specs=[near] * count,
        out_specs=[anywhere] * count,
        scratch_shapes=[pltpu.SemaphoreType.DMA((count,))],
    )(*[pltpu.with_memory_space_constraint(out, pltpu.VMEM) for out in outs])
    weights, master_new, first_q_new, first_scale_new, second_q_new, second_scale_new = outs
    return (
        weights,
        master_new,
        first_q_new,
        first_scale_new.reshape(own),
        second_q_new,
        second_scale_new.reshape(own),
    )


def solution(mesh):
    placed = (P("dp", None, None), P("dp", None), P("dp", None), P("dp"), P("dp", None), P("dp"))
    return jax.shard_map(
        shards,
        mesh=mesh,
        in_specs=placed,
        out_specs=(P(), P("dp", None), P("dp", None), P("dp"), P("dp", None), P("dp")),
        check_vma=False,
    )
```
